32 devices in a mesh: seq: 8 (over y, x, core), head: 4 (over z).
Axes of the slice: x: 2, y: 2, z: 4, core: 2. Of those that a mesh axis runs over, the one named last changes fastest.
Arguments:
- mixer_input: bfloat16 [12288, 4096], P('seq', 'head'), may hold values from -6 to 6
- gate_input: bfloat16 [12288, 4096], P('seq', 'head'), may hold values from -6 to 6
- state_maps: bfloat16 [4, 12288, 128], P(None, 'seq'), may hold values from -0.375 to 0.375
- step_size: float32 [2, 64, 12288], P(None, 'head', 'seq'), may hold values from 0.2 to 2
- log_decay: float32 [2, 64, 12288], P(None, 'head', 'seq'), may hold values from -2 to 0
- skip_weight: float32 [64], P('head'), may hold values from 0.5 to 1.5
- doc_ids: int32 [12288], P('seq'), may hold values from 0 to 3, never falling along the last dimension, each value on 1 to 6144 neighbouring positions
- norm_gain: float32 [4096], P('head'), may hold values from 0.1 to 1.9
Outputs:
- mixed: bfloat16 [12288, 4096], P('seq', 'head')
The draws below stay inside these ranges and needn't reach their ends.
Inputs may be any that keep to these rules, and one draw needn't show every extreme that they name: `doc_ids`: ids never fall along the sequence; each of the 4 documents holds 1 to 6144 tokens, one exactly 6144.
All inputs are finite; a program needn't handle non-finite values.
Results may differ from the reference program's by a relative error of at most 0.0054.
Values sent between devices are 32-bit elements; how exact they have to be, the bound alone decides.
A program may use at most 256 MiB of HBM per device.

```python
import math
import jax
import jax.numpy as jnp
import numpy as np
from jax import lax

HEADDIM = 64
NSTATE = 128
BLOCK = 128
DOCS = 4
TOK_DEV = 1536
HEADS = 64
LENGTH = 12288
N_HEAD = 4


def draw_gate_input(key, part):
    channel = jnp.arange(HEADS * HEADDIM) // HEADDIM
    rising = 0.6 * (1.0 + 2.0 * channel.astype(jnp.float32) / max(HEADS - 1, 1))
    base = jax.random.normal(key, (LENGTH, HEADS * HEADDIM), jnp.float32)
    return jnp.clip(base * rising[None, :], -6.0, 6.0).astype(jnp.bfloat16)


def draw_log_decay(key, part):
    keys = jax.random.split(key, 7)
    slow_share = 0.5
    slow_heads = jax.random.bernoulli(keys[0], slow_share, (2, HEADS, 1))
    fast_rate = jnp.exp(jax.random.uniform(keys[1], (2, HEADS, 1), jnp.float32, math.log(1.0 / 50.0), math.log(1.0 / 30.0)))
    slow_rate = jnp.exp(jax.random.uniform(keys[2], (2, HEADS, 1), jnp.float32, math.log(0.05), math.log(0.1))) / LENGTH
    forgetting_speeds = jnp.where(slow_heads, slow_rate, fast_rate)
    hardware_scaling_factor = jnp.exp(jax.random.uniform(keys[3], (2, HEADS, LENGTH // TOK_DEV), jnp.float32, 0.0, math.log(3.0)))
    hardware_scaling_factor = jnp.repeat(hardware_scaling_factor, TOK_DEV, axis=2)
    exterior_unevenness = jax.random.uniform(keys[4], (2, HEADS, LENGTH), jnp.float32, 0.5, 1.5)
    flagged_spots = jax.random.randint(keys[5], (2, 2), 0, LENGTH)
    layer_tiers = jax.random.uniform(keys[6], (2, 2), jnp.float32, 0.22, 0.69)
    sequence_offsets = jnp.arange(LENGTH)
    spike_occurrences = jnp.sum(jnp.where(sequence_offsets[None, None, :] == flagged_spots[:, :, None], layer_tiers[:, :, None], 0.0), axis=1)
    return -(forgetting_speeds * hardware_scaling_factor * exterior_unevenness) - spike_occurrences[:, None, :]


def block_scale(key, dims, cuts, low, high):
    def one(axis_at, blocks):
        draws = jax.random.uniform(jax.random.fold_in(jax.random.fold_in(key, 6), axis_at), (blocks,), jnp.float32, low / len(cuts), high / len(cuts))
        return jnp.repeat(jnp.exp(draws), dims[axis_at] // blocks).reshape((-1,) + (1,) * (len(dims) - axis_at - 1))

    gain = one(*cuts[0])
    for cut in cuts[1:]:
        gain = gain * one(*cut)
    return gain


def profile(count, total, bound, skew):
    loads = [(1 << 20) // math.isqrt(rank ** skew) + 1 for rank in range(2, count + 1)]
    rest, holding = total - bound - (count - 1), [1] * (count - 1)
    while rest > 0:
        movable = [i for i in range(count - 1) if holding[i] < bound]
        mass, budget = sum([loads[i] for i in movable]), rest
        for i in movable:
            extra = min(bound - holding[i], max(1, budget * loads[i] // mass), rest)
            holding[i] = holding[i] + extra
            rest = rest - extra
    return np.array([bound] + holding)


def uneven(key, amount, total, reach, slope):
    if amount == 2:
        one = jax.random.randint(key, (), max(1, total - reach), min(reach, total - 1) + 1)
        return jnp.stack([one, total - one])
    sizes = jnp.asarray(profile(amount, total, reach, slope), jnp.int32)
    twos = (amount - 1) // 2
    source_of, sink = sizes[1:1 + 2 * twos:2], sizes[2:2 + 2 * twos:2]
    room = jnp.minimum(source_of - 1, reach - sink)
    moved = jax.random.randint(jax.random.fold_in(key, 1), (twos,), 0, 1 << 20) % (room + 1)
    sizes = sizes.at[1:1 + 2 * twos:2].set(source_of - moved).at[2:2 + 2 * twos:2].set(sink + moved)
    return sizes[jax.random.permutation(jax.random.fold_in(key, 2), amount)]


def bell_draw(own_key, dims, deviation, reach, shards=(), kind=jnp.bfloat16):
    drawn = jax.random.normal(own_key, dims, jnp.float32) * deviation
    if len(shards) > 0:
        drawn = block_scale(own_key, dims, shards, -0.22, 0.18) * drawn
    return jnp.clip(drawn, min=-reach, max=reach).astype(kind)


def setup_inputs(seed: int = 0) -> dict:
    key_list = jax.random.split(jax.random.key(seed), 9)
    mixer_input = bell_draw(key_list[0], (LENGTH, HEADS * HEADDIM), 1.0, 6.0, ((0, 8), (1, 4)))
    gate_input = draw_gate_input(jax.random.fold_in(key_list[8], 71), 0)
    state_maps = bell_draw(key_list[2], (4, LENGTH, NSTATE), (0.2 * NSTATE ** -0.25), 0.375, ((1, 8),))
    step_size = jnp.clip(0.2 + 1.8 * jax.random.uniform(key_list[3], (2, HEADS, LENGTH), jnp.float32) ** block_scale(key_list[3], (2, HEADS, LENGTH), ((1, 4), (2, 8)), -0.2, 0.2), 0.2, 2.0)
    log_decay = draw_log_decay(jax.random.fold_in(key_list[8], 71), 0)
    skip_weight = jnp.clip(0.5 + 1.0 * jax.random.uniform(key_list[5], (HEADS,), jnp.float32) ** block_scale(key_list[5], (HEADS,), ((0, 4),), -0.2, 0.2), 0.5, 1.5)
    doc_ids = jnp.searchsorted(jnp.cumsum(uneven(key_list[6], DOCS, LENGTH, LENGTH // 2, 0)), jnp.arange(LENGTH), side="right").astype(jnp.int32)
    norm_gain = jnp.clip(1.0 + 0.18 * jax.random.normal(key_list[7], (HEADS * HEADDIM,), jnp.float32), 0.1, 1.9)
    return {"mixer_input": mixer_input, "gate_input": gate_input, "state_maps": state_maps, "step_size": step_size, "log_decay": log_decay, "skip_weight": skip_weight, "doc_ids": doc_ids, "norm_gain": norm_gain}


def one_direction(values, b_rows, c_rows, decay_rows, step_rows, doc_rows):
    length = values.shape[0]
    block_count = length // BLOCK
    head_count = decay_rows.shape[0]
    sequence = (values.reshape(block_count, BLOCK, head_count, HEADDIM), b_rows.reshape(block_count, BLOCK, NSTATE), c_rows.reshape(block_count, BLOCK, NSTATE), decay_rows.reshape(head_count, block_count, BLOCK).transpose(1, 0, 2), step_rows.reshape(head_count, block_count, BLOCK).transpose(1, 0, 2), doc_rows.reshape(block_count, BLOCK))

    def advance(carried_pair, block_item):
        state_now, prior_id = carried_pair
        block_x, block_b, block_c, block_decay, block_step, block_docs = block_item
        cumulative = jnp.cumsum(block_decay, axis=1)
        scores = jnp.dot(block_c, block_b.T, preferred_element_type=jnp.float32)
        places = jnp.arange(BLOCK)
        strict = (places[:, None] > places[None, :]) & (block_docs[:, None] == block_docs[None, :])
        spread = jnp.where(strict[None], cumulative[:, :, None] - cumulative[:, None, :], 0.0)
        weights = jnp.where(strict[None], scores[None] * jnp.exp(spread) * block_step[:, None, :], 0.0)
        weights = lax.optimization_barrier(weights.astype(jnp.bfloat16)).astype(jnp.float32)
        values_wide = block_x.astype(jnp.float32)
        inside_out = jnp.einsum('hts,shp->thp', weights, values_wide, precision=lax.Precision.HIGHEST)
        entering = lax.optimization_barrier(state_now.astype(jnp.bfloat16)).astype(jnp.float32)
        carried = jnp.einsum('tn,hnp->thp', block_c.astype(jnp.float32), entering, precision=lax.Precision.HIGHEST)
        carry_reach = jnp.exp(cumulative).T * (block_docs == prior_id).astype(jnp.float32)[:, None]
        last_id = block_docs[BLOCK - 1]
        to_end = jnp.where((block_docs == last_id)[None], jnp.exp(cumulative[:, -1:] - cumulative) * block_step, 0.0)
        weighted_b = (block_b.astype(jnp.float32)[None] * to_end[:, :, None]).astype(jnp.bfloat16)
        weighted_b = lax.optimization_barrier(weighted_b).astype(jnp.float32)
        local_state = jnp.einsum('hsn,shp->hnp', weighted_b, values_wide, precision=lax.Precision.HIGHEST)
        keeping = (last_id == prior_id).astype(jnp.float32)
        state_next = (jnp.exp(cumulative[:, -1]) * keeping)[:, None, None] * state_now + local_state
        return ((state_next, last_id), inside_out + carried * carry_reach[:, :, None])
    start_state = jnp.zeros((head_count, NSTATE, HEADDIM), jnp.float32)
    final_pair, outputs = lax.scan(advance, (start_state, doc_rows[0]), sequence)
    return outputs.reshape(length, head_count, HEADDIM)

def reference(mixer_input, gate_input, state_maps, step_size, log_decay, skip_weight, doc_ids, norm_gain):
    groups = N_HEAD
    group_heads = HEADS // groups
    value_group = mixer_input.reshape(LENGTH, groups, group_heads, HEADDIM).transpose(1, 0, 2, 3)
    gate_group = gate_input.reshape(LENGTH, groups, group_heads * HEADDIM).transpose(1, 0, 2)
    step_group = step_size.reshape(2, groups, group_heads, LENGTH).transpose(1, 0, 2, 3)
    decay_group = log_decay.reshape(2, groups, group_heads, LENGTH).transpose(1, 0, 2, 3)
    skip_group = skip_weight.reshape(groups, group_heads)
    reversed_docs = doc_ids[::-1]

    def per_group(group_item):
        values, gates, steps_here, decays_here, skips_here = group_item
        forward_out = one_direction(values, state_maps[0], state_maps[1], decays_here[0], steps_here[0], doc_ids)
        backward_out = one_direction(values[::-1], state_maps[2][::-1], state_maps[3][::-1], decays_here[1][:, ::-1], steps_here[1][:, ::-1], reversed_docs)[::-1]
        combined = forward_out + backward_out + skips_here[None, :, None] * values.astype(jnp.float32)
        gate_wide = gates.astype(jnp.float32).reshape(combined.shape)
        gated_out = (combined * jax.nn.silu(gate_wide)).reshape(LENGTH, group_heads * HEADDIM)
        return (gated_out, lax.optimization_barrier(jnp.sum(gated_out * gated_out, axis=1)))
    gated_all, squares = lax.map(per_group, (value_group, gate_group, step_group, decay_group, skip_group))
    square_total = lax.optimization_barrier(jnp.sum(squares, axis=0))
    inverse_rms = lax.rsqrt(square_total / (HEADS * HEADDIM) + 1e-05)
    scaled = (gated_all * inverse_rms[None, :, None]).transpose(1, 0, 2).reshape(LENGTH, HEADS * HEADDIM)
    return (scaled * norm_gain[None, :]).astype(jnp.bfloat16)
```

```python
import functools

import jax
import jax.numpy as jnp
from jax import lax
from jax.experimental import pallas as pl
from jax.experimental.pallas import tpu as pltpu
from jax.sharding import PartitionSpec as P

BLOCK = 128
ROWS = 136
F32 = jnp.float32
BF16 = jnp.bfloat16
HIGH = lax.Precision.HIGHEST


def iota(shape, axis):
    return lax.broadcasted_iota(jnp.int32, shape, axis)


def spread(columns, first, heads):
    rows = columns.shape[0]
    half = iota((rows, 128), 1) // 64
    parts = []
    for pair in range(heads // 2):
        index = first + 2 * pair + half
        parts.append(jnp.take_along_axis(columns, index, axis=1, mode="promise_in_bounds"))
    return jnp.concatenate(parts, axis=1)


def kernel(
    sizes, x_ref, gate_ref, maps_ref, step_ref, decay_ref, skip_ref, docs_ref, gain_ref, out_ref,
    own, other, total, slots, into, local, columns, rows, reach, state, state16, acc, squares, inverse,
    send_a, recv_a, send_b, recv_b, send_c, recv_c, send_h, recv_h,
):
    seq, head_ways, heads = sizes
    chips = seq // 2
    width = heads * 64
    half = width // 2
    blocks = x_ref.shape[0] // BLOCK
    place = lax.axis_index("seq")
    core = lax.rem(place, 2)
    chip = lax.div(place, 2)
    head_place = lax.axis_index("head")
    sibling = place + 1 - 2 * core

    def chip_at(offset):
        return {"seq": 2 * lax.rem(chip + offset, chips) + core}

    def head_at(offset):
        return {"head": lax.rem(head_place + offset, head_ways)}

    barrier = pltpu.get_barrier_semaphore()
    partners = [{"seq": sibling}]
    partners += [chip_at(o) for o in range(1, chips)] + [head_at(o) for o in range(1, head_ways)]
    for partner in partners:
        pl.semaphore_signal(barrier, inc=1, device_id=partner, device_id_type=pl.DeviceIdType.MESH)
    pl.semaphore_wait(barrier, len(partners))

    def remote(src, dst, send, recv, device):
        return pltpu.make_async_remote_copy(
            src_ref=src, dst_ref=dst, send_sem=send, recv_sem=recv,
            device_id=device, device_id_type=pl.DeviceIdType.MESH,
        )

    below = (iota((BLOCK, BLOCK), 0) <= iota((BLOCK, BLOCK), 1)).astype(F32)
    above = (iota((BLOCK, BLOCK), 0) >= iota((BLOCK, BLOCK), 1)).astype(F32)
    tile = iota((8, half), 0)

    def at(k):
        return pl.ds(pl.multiple_of(k * BLOCK, BLOCK), BLOCK)

    state[...] = jnp.zeros_like(state)
    first_doc = docs_ref[0:1, 0:1]
    last_doc = docs_ref[blocks - 1 : blocks, BLOCK - 1 : BLOCK]

    def summarize(k, carry):
        log_f, log_b, prior = carry
        docs = docs_ref[pl.ds(k, 1), :]
        first, last = docs[:, :1], docs[:, BLOCK - 1 :]
        cum_f = jnp.dot(decay_ref[0, :, at(k)], below, precision=HIGH, preferred_element_type=F32)
        cum_b = jnp.dot(decay_ref[1, :, at(k)], above, precision=HIGH, preferred_element_type=F32)
        step_f, step_b = step_ref[0, :, at(k)], step_ref[1, :, at(k)]
        in_f = jnp.where(docs == last, jnp.exp(cum_f[:, BLOCK - 1 :] - cum_f) * step_f, 0.0)
        in_b = jnp.where(docs == first, jnp.exp(cum_b[:, :1] - cum_b) * step_b, 0.0)
        pad = jnp.zeros((BLOCK - 4 * heads, BLOCK), F32)
        cols = jnp.concatenate([cum_f, cum_b, in_f, in_b, pad], axis=0).T
        columns[at(k), :] = cols
        rows[k, 0] = cum_f - jnp.log(step_f)
        rows[k, 1] = cum_b - jnp.log(step_b)
        reach[k, 0] = cum_f
        reach[k, 1] = cum_b
        x = x_ref[at(k), :].astype(F32)
        put_f = (x * spread(cols, 2 * heads, heads)).astype(BF16)
        put_b = (x * spread(cols, 3 * heads, heads)).astype(BF16)
        map_f = maps_ref[0, at(k), :].astype(F32).T.astype(BF16)
        map_b = maps_ref[2, at(k), :].astype(F32).T.astype(BF16)
        local_f = jnp.dot(map_f, put_f, preferred_element_type=F32)
        local_b = jnp.dot(map_b, put_b, preferred_element_type=F32)
        local[0, k] = local_f
        local[1, k] = local_b
        block_f = spread(cols[BLOCK - 8 :], 0, heads)[7:]
        block_b = spread(cols[:8], heads, heads)[:1]
        keep = jnp.exp(block_f) * (prior == last).astype(F32)
        state[0] = state[0] * keep + local_f
        state[1] = state[1] + local_b * (jnp.exp(log_b) * (first == first_doc).astype(F32))
        return log_f + block_f, log_b + block_b, last

    zero = jnp.zeros((1, width), F32)
    logs = lax.fori_loop(0, blocks, summarize, (zero, zero, jnp.full((1, 1), -1.0, F32)))
    for g in range(2):
        part = slice(g * half, (g + 1) * half)
        for d, doc in ((0, last_doc), (1, first_doc)):
            own[g, d, 0:128, :] = state[d, :, part]
            own[g, d, 128:ROWS, :] = jnp.where(tile == 0, logs[d][:, part], doc)

    to_sibling = remote(own, other, send_a, recv_a, {"seq": sibling})
    to_sibling.start()

    low = iota((BLOCK, BLOCK), 1) < iota((BLOCK, BLOCK), 0)
    diagonal = iota((BLOCK, BLOCK), 1) == iota((BLOCK, BLOCK), 0)
    left = iota((BLOCK, BLOCK), 1) < 64

    def inside(k, carry):
        docs = jnp.broadcast_to(docs_ref[pl.ds(k, 1), :], (BLOCK, BLOCK))
        dims = (((1,), (1,)), ((), ()))
        score_f = lax.dot_general(maps_ref[1, at(k), :], maps_ref[0, at(k), :], dims, preferred_element_type=F32)
        score_b = lax.dot_general(maps_ref[3, at(k), :], maps_ref[2, at(k), :], dims, preferred_element_type=F32)
        same = (docs == docs.T) & jnp.logical_not(diagonal)
        score = jnp.where(same, jnp.where(low, score_f, score_b), 0.0)
        cols = columns[at(k), :]
        row_f, row_b = rows[k, 0], rows[k, 1]
        for pair in range(heads // 2):
            lanes = slice(pair * 128, pair * 128 + 128)
            x = x_ref[at(k), lanes]
            weights = []
            for h in (2 * pair, 2 * pair + 1):
                power = jnp.where(
                    low,
                    cols[:, h : h + 1] - row_f[h : h + 1],
                    cols[:, heads + h : heads + h + 1] - row_b[h : h + 1],
                )
                weights.append((score * jnp.exp(power)).astype(BF16))
            none = jnp.zeros_like(x)
            values = jnp.concatenate([jnp.where(left, x, none), jnp.where(left, none, x)], axis=0)
            acc[at(k), lanes] = jnp.dot(
                jnp.concatenate(weights, axis=1), values, preferred_element_type=F32
            )
        return carry

    cut_a, cut_b = blocks // 4, blocks - blocks // 6
    lax.fori_loop(0, cut_a, inside, 0)
    to_sibling.wait()

    def join(later, earlier):
        log, doc = later[128:129], later[129:130]
        keep = jnp.exp(log) * (doc == earlier[129:130]).astype(F32)
        top = later[0:128] + keep * earlier[0:128]
        return top, jnp.where(tile == 0, log + earlier[128:129], doc)

    @pl.when(core == 0)
    def _():
        for d, (later, earlier) in ((0, (other, own)), (1, (own, other))):
            top, end = join(later[0, d], earlier[0, d])
            total[d, 0:128, :] = top
            total[d, 128:ROWS, :] = end

    @pl.when(core == 1)
    def _():
        for d, (later, earlier) in ((0, (own, other)), (1, (other, own))):
            top, end = join(later[1, d], earlier[1, d])
            total[d, 0:128, :] = top
            total[d, 128:ROWS, :] = end

    to_chips = []
    for o in range(1, chips):
        way = jnp.where(chip + o < chips, 0, 1)
        to_chips.append(remote(total.at[way], slots.at[o], send_b.at[o], recv_b.at[o], chip_at(o)))
        to_chips[-1].start()
    lax.fori_loop(cut_a, cut_b, inside, 0)
    for copy in to_chips:
        copy.wait()

    for d in range(2):
        into[core, d, 0:128, :] = jnp.zeros((128, half), F32)
        into[core, d, 128:ROWS, :] = jnp.where(tile == 0, 0.0, -1.0)
        for o in range(1, chips):
            slot = o if d == 0 else chips - o
            there = chip >= o if d == 0 else chip + o < chips

            @pl.when(there)
            def _(d=d, o=o, slot=slot):
                part = slots[slot]
                log, doc = part[128:129], part[129:130]
                if o == 1:
                    into[core, d] = part
                else:
                    so_far = into[core, d, 128:ROWS, :]
                    keep = jnp.exp(so_far[0:1]) * (doc == so_far[1:2]).astype(F32)
                    into[core, d, 0:128, :] += keep * part[0:128]
                    into[core, d, 128:ROWS, :] = jnp.where(tile == 0, so_far[0:1] + log, so_far[1:2])

    share = remote(into.at[core], into.at[core], send_c, recv_c, {"seq": sibling})
    share.start()
    lax.fori_loop(cut_b, blocks, inside, 0)
    share.wait_send()
    remote(into.at[core], into.at[1 - core], send_c, recv_c, {"seq": sibling}).wait_recv()

    for d in range(2):
        for g in range(2):
            part = slice(g * half, (g + 1) * half)

            @pl.when(core == d)
            def _(d=d, g=g, part=part):
                state[d, :, part] = into[g, d, 0:128, :]
                if g == 0:
                    state16[d] = into[g, d, 128:ROWS, 0:128]

            @pl.when(core != d)
            def _(d=d, g=g, part=part):
                top, end = join(other[g, d], into[g, d])
                state[d, :, part] = top
                if g == 0:
                    state16[d] = end[:, 0:128]

    def leave(d, k, prior):
        docs = docs_ref[pl.ds(k, 1), :]
        cum = reach[k, d]
        carry = jnp.where(docs == prior, jnp.exp(cum), 0.0)
        cols = jnp.concatenate([carry, cum, jnp.zeros((BLOCK - 2 * heads, BLOCK), F32)], axis=0).T
        before = state[d]
        given = jnp.dot(maps_ref[2 * d + 1, at(k), :], before.astype(BF16), preferred_element_type=F32)
        if d == 0:
            block, last = spread(cols[BLOCK - 8 :], heads, heads)[7:], docs[:, BLOCK - 1 :]
        else:
            block, last = spread(cols[:8], heads, heads)[:1], docs[:, :1]
        state[d] = before * (jnp.exp(block) * (last == prior).astype(F32)) + local[d, k]
        return given * spread(cols, 0, heads), last

    def forward(k, prior):
        part, last = leave(0, k, prior)
        acc[at(k), :] += part
        return last

    lax.fori_loop(0, blocks, forward, state16[0, 1:2, 0:1])
    squares[0] = jnp.zeros((BLOCK, 128), F32)
    lane = iota((BLOCK, 128), 1)

    def backward(step, prior):
        k = blocks - 1 - step
        part, last = leave(1, k, prior)
        gate = gate_ref[at(k), :].astype(F32)
        mixed = acc[at(k), :] + part + skip_ref[...] * x_ref[at(k), :].astype(F32)
        gated = mixed * (gate / (1.0 + jnp.exp(-gate)))
        acc[at(k), :] = gated
        squares[0] += jnp.where(lane == k, jnp.sum(gated * gated, axis=1, keepdims=True), 0.0)
        return last

    lax.fori_loop(0, blocks, backward, state16[1, 1:2, 0:1])
    to_heads = [
        remote(squares.at[0], squares.at[o], send_h.at[o], recv_h.at[o], head_at(o))
        for o in range(1, head_ways)
    ]
    for copy in to_heads:
        copy.start()
    for copy in to_heads:
        copy.wait()
    sum_all = squares[0]
    for o in range(1, head_ways):
        sum_all = sum_all + squares[o]
    inverse[...] = lax.rsqrt(sum_all / (head_ways * width) + 1e-05)

    def scale(k, carry):
        factor = jnp.sum(jnp.where(lane == k, inverse[...], 0.0), axis=1, keepdims=True)
        out_ref[at(k), :] = (acc[at(k), :] * factor * gain_ref[...]).astype(BF16)
        return carry

    lax.fori_loop(0, blocks, scale, 0)


def local(
    mixer_input, gate_input, state_maps, step_size, log_decay, skip_weight, doc_ids, norm_gain
):
    tokens, width = mixer_input.shape
    heads = step_size.shape[1]
    blocks = tokens // BLOCK
    half = width // 2
    seq, head_ways = lax.axis_size("seq"), lax.axis_size("head")
    chips = seq // 2
    docs = doc_ids.reshape(blocks, BLOCK).astype(F32)
    skip = jnp.repeat(skip_weight, width // heads)[None, :]
    vmem = pl.BlockSpec(memory_space=pltpu.VMEM)
    return pl.pallas_call(
        functools.partial(kernel, (seq, head_ways, heads)),
        out_shape=jax.ShapeDtypeStruct((tokens, width), BF16),
        in_specs=[vmem] * 8,
        out_specs=vmem,
        scratch_shapes=[
            pltpu.VMEM((2, 2, ROWS, half), F32),
            pltpu.VMEM((2, 2, ROWS, half), F32),
            pltpu.VMEM((2, ROWS, half), F32),
            pltpu.VMEM((chips, ROWS, half), F32),
            pltpu.VMEM((2, 2, ROWS, half), F32),
            pltpu.VMEM((2, blocks, 128, width), F32),
            pltpu.VMEM((tokens, 128), F32),
            pltpu.VMEM((blocks, 2, heads, 128), F32),
            pltpu.VMEM((blocks, 2, heads, 128), F32),
            pltpu.VMEM((2, 128, width), F32),
            pltpu.VMEM((2, 8, 128), F32),
            pltpu.VMEM((tokens, width), F32),
            pltpu.VMEM((head_ways, BLOCK, 128), F32),
            pltpu.VMEM((BLOCK, 128), F32),
            pltpu.SemaphoreType.DMA,
            pltpu.SemaphoreType.DMA,
            pltpu.SemaphoreType.DMA((chips,)),
            pltpu.SemaphoreType.DMA((chips,)),
            pltpu.SemaphoreType.DMA,
            pltpu.SemaphoreType.DMA,
            pltpu.SemaphoreType.DMA((head_ways,)),
            pltpu.SemaphoreType.DMA((head_ways,)),
        ],
        compiler_params=pltpu.CompilerParams(
            collective_id=0, has_side_effects=True, vmem_limit_bytes=56 * 2**20
        ),
    )(mixer_input, gate_input, state_maps, step_size, log_decay, skip, docs, norm_gain[None, :])


def solution(mesh):
    return jax.shard_map(
        local,
        mesh=mesh,
        in_specs=(
            P("seq", "head"),
            P("seq", "head"),
            P(None, "seq", None),
            P(None, "head", "seq"),
            P(None, "head", "seq"),
            P("head"),
            P("seq"),
            P("head"),
        ),
        out_specs=P("seq", "head"),
        check_vma=False,
    )
```

```python
import functools

import jax
import jax.numpy as jnp
from jax import lax
from jax.experimental import pallas as pl
from jax.experimental.pallas import tpu as pltpu
from jax.sharding import PartitionSpec as P

BLOCK = 128
ROWS = 136
F32 = jnp.float32
BF16 = jnp.bfloat16
HIGH = lax.Precision.HIGHEST


def iota(shape, axis):
    return lax.broadcasted_iota(jnp.int32, shape, axis)


def spread(columns, first, heads):
    rows = columns.shape[0]
    half = iota((rows, 128), 1) // 64
    parts = []
    for pair in range(heads // 2):
        index = first + 2 * pair + half
        parts.append(jnp.take_along_axis(columns, index, axis=1, mode="promise_in_bounds"))
    return jnp.concatenate(parts, axis=1)


def kernel(
    sizes, x_ref, gate_ref, maps_ref, step_ref, decay_ref, skip_ref, docs_ref, gain_ref, out_ref,
    own, other, total, slots, into, local, columns, rows, gains, state, acc, squares, inverse,
    send_a, recv_a, send_b, recv_b, send_c, recv_c, send_h, recv_h,
):
    seq, head_ways, heads = sizes
    chips = seq // 2
    width = heads * 64
    half = width // 2
    blocks = x_ref.shape[0] // BLOCK
    place = lax.axis_index("seq")
    core = lax.rem(place, 2)
    chip = lax.div(place, 2)
    head_place = lax.axis_index("head")
    sibling = place + 1 - 2 * core

    def chip_at(offset):
        return {"seq": 2 * lax.rem(chip + offset, chips) + core}

    def head_at(offset):
        return {"head": lax.rem(head_place + offset, head_ways)}

    barrier = pltpu.get_barrier_semaphore()
    partners = [{"seq": sibling}]
    partners += [chip_at(o) for o in range(1, chips)] + [head_at(o) for o in range(1, head_ways)]
    for partner in partners:
        pl.semaphore_signal(barrier, inc=1, device_id=partner, device_id_type=pl.DeviceIdType.MESH)
    pl.semaphore_wait(barrier, len(partners))

    def remote(src, dst, send, recv, device):
        return pltpu.make_async_remote_copy(
            src_ref=src, dst_ref=dst, send_sem=send, recv_sem=recv,
            device_id=device, device_id_type=pl.DeviceIdType.MESH,
        )

    below = (iota((BLOCK, BLOCK), 0) <= iota((BLOCK, BLOCK), 1)).astype(F32)
    above = (iota((BLOCK, BLOCK), 0) >= iota((BLOCK, BLOCK), 1)).astype(F32)
    tile = iota((8, half), 0)

    def at(k):
        return pl.ds(pl.multiple_of(k * BLOCK, BLOCK), BLOCK)

    state[...] = jnp.zeros_like(state)
    first_doc = docs_ref[0:1, :].astype(F32)[:, :1]
    last_doc = docs_ref[blocks - 1 : blocks, :].astype(F32)[:, BLOCK - 1 :]

    def summarize(k, carry):
        log_f, log_b, prior = carry
        docs = docs_ref[pl.ds(k, 1), :].astype(F32)
        after = docs_ref[pl.ds(jnp.minimum(k + 1, blocks - 1), 1), :].astype(F32)
        first, last = docs[:, :1], docs[:, BLOCK - 1 :]
        after = jnp.where(k == blocks - 1, last, after[:, :1])
        cum_f = jnp.dot(decay_ref[0, :, at(k)], below, precision=HIGH, preferred_element_type=F32)
        cum_b = jnp.dot(decay_ref[1, :, at(k)], above, precision=HIGH, preferred_element_type=F32)
        step_f, step_b = step_ref[0, :, at(k)], step_ref[1, :, at(k)]
        in_f = jnp.where(docs == last, jnp.exp(cum_f[:, BLOCK - 1 :] - cum_f) * step_f, 0.0)
        in_b = jnp.where(docs == first, jnp.exp(cum_b[:, :1] - cum_b) * step_b, 0.0)
        out_f = jnp.where(docs == prior, jnp.exp(cum_f), 0.0)
        out_b = jnp.where(docs == after, jnp.exp(cum_b), 0.0)
        pad = jnp.zeros((BLOCK - 6 * heads, BLOCK), F32)
        cols = jnp.concatenate([cum_f, cum_b, in_f, in_b, out_f, out_b, pad], axis=0).T
        columns[at(k), :] = cols
        rows[k, 0] = cum_f - jnp.log(step_f)
        rows[k, 1] = cum_b - jnp.log(step_b)
        x = x_ref[at(k), :].astype(F32)
        put_f = (x * spread(cols, 2 * heads, heads)).astype(BF16)
        put_b = (x * spread(cols, 3 * heads, heads)).astype(BF16)
        map_f = maps_ref[0, at(k), :].astype(F32).T.astype(BF16)
        map_b = maps_ref[2, at(k), :].astype(F32).T.astype(BF16)
        local_f = jnp.dot(map_f, put_f, preferred_element_type=F32)
        local_b = jnp.dot(map_b, put_b, preferred_element_type=F32)
        local[0, k] = local_f
        local[1, k] = local_b
        block_f = spread(cols[BLOCK - 8 :], 0, heads)[7:]
        block_b = spread(cols[:8], heads, heads)[:1]
        keep = jnp.exp(block_f) * (prior == last).astype(F32)
        gains[k, 0:1, :] = keep
        gains[k, 1:2, :] = jnp.exp(block_b) * (after == first).astype(F32)
        state[0] = state[0] * keep + local_f
        state[1] = state[1] + local_b * (jnp.exp(log_b) * (first == first_doc).astype(F32))
        return log_f + block_f, log_b + block_b, last

    zero = jnp.zeros((1, width), F32)
    logs = lax.fori_loop(0, blocks, summarize, (zero, zero, first_doc))
    for g in range(2):
        part = slice(g * half, (g + 1) * half)
        for d, doc in ((0, last_doc), (1, first_doc)):
            own[g, d, 0:128, :] = state[d, :, part]
            own[g, d, 128:ROWS, :] = jnp.where(tile == 0, logs[d][:, part], doc)

    to_sibling = remote(own, other, send_a, recv_a, {"seq": sibling})
    to_sibling.start()

    low = iota((BLOCK, BLOCK), 1) < iota((BLOCK, BLOCK), 0)
    diagonal = iota((BLOCK, BLOCK), 1) == iota((BLOCK, BLOCK), 0)
    left = iota((BLOCK, BLOCK), 1) < 64

    def inside(k, carry):
        docs = jnp.broadcast_to(docs_ref[pl.ds(k, 1), :].astype(F32), (BLOCK, BLOCK))
        dims = (((1,), (1,)), ((), ()))
        score_f = lax.dot_general(maps_ref[1, at(k), :], maps_ref[0, at(k), :], dims, preferred_element_type=F32)
        score_b = lax.dot_general(maps_ref[3, at(k), :], maps_ref[2, at(k), :], dims, preferred_element_type=F32)
        same = (docs == docs.T) & jnp.logical_not(diagonal)
        score = jnp.where(same, jnp.where(low, score_f, score_b), 0.0)
        cols = columns[at(k), :]
        row_f, row_b = rows[k, 0], rows[k, 1]
        for pair in range(heads // 2):
            lanes = slice(pair * 128, pair * 128 + 128)
            x = x_ref[at(k), lanes]
            weights = []
            for h in (2 * pair, 2 * pair + 1):
                power = jnp.where(
                    low,
                    cols[:, h : h + 1] - row_f[h : h + 1],
                    cols[:, heads + h : heads + h + 1] - row_b[h : h + 1],
                )
                weights.append((score * jnp.exp(power)).astype(BF16))
            none = jnp.zeros_like(x)
            values = jnp.concatenate([jnp.where(left, x, none), jnp.where(left, none, x)], axis=0)
            acc[at(k), lanes] = jnp.dot(
                jnp.concatenate(weights, axis=1), values, preferred_element_type=F32
            )
        return carry

    cut_a, cut_b = blocks // 4, blocks - blocks // 6
    lax.fori_loop(0, cut_a, inside, 0)
    to_sibling.wait()

    def join(later, earlier):
        log, doc = later[128:129], later[129:130]
        keep = jnp.exp(log) * (doc == earlier[129:130]).astype(F32)
        top = later[0:128] + keep * earlier[0:128]
        return top, jnp.where(tile == 0, log + earlier[128:129], doc)

    @pl.when(core == 0)
    def _():
        for d, (later, earlier) in ((0, (other, own)), (1, (own, other))):
            top, end = join(later[0, d], earlier[0, d])
            total[d, 0:128, :] = top
            total[d, 128:ROWS, :] = end

    @pl.when(core == 1)
    def _():
        for d, (later, earlier) in ((0, (own, other)), (1, (other, own))):
            top, end = join(later[1, d], earlier[1, d])
            total[d, 0:128, :] = top
            total[d, 128:ROWS, :] = end

    to_chips = []
    for o in range(1, chips):
        way = jnp.where(chip + o < chips, 0, 1)
        to_chips.append(remote(total.at[way], slots.at[o], send_b.at[o], recv_b.at[o], chip_at(o)))
        to_chips[-1].start()
    lax.fori_loop(cut_a, cut_b, inside, 0)
    for copy in to_chips:
        copy.wait()

    for d in range(2):
        into[core, d, 0:128, :] = jnp.zeros((128, half), F32)
        into[core, d, 128:ROWS, :] = jnp.where(tile == 0, 0.0, -1.0)
        for o in range(1, chips):
            slot = o if d == 0 else chips - o
            there = chip >= o if d == 0 else chip + o < chips

            @pl.when(there)
            def _(d=d, o=o, slot=slot):
                part = slots[slot]
                log, doc = part[128:129], part[129:130]
                if o == 1:
                    into[core, d] = part
                else:
                    so_far = into[core, d, 128:ROWS, :]
                    keep = jnp.exp(so_far[0:1]) * (doc == so_far[1:2]).astype(F32)
                    into[core, d, 0:128, :] += keep * part[0:128]
                    into[core, d, 128:ROWS, :] = jnp.where(tile == 0, so_far[0:1] + log, so_far[1:2])

    share = remote(into.at[core], into.at[core], send_c, recv_c, {"seq": sibling})
    share.start()
    lax.fori_loop(cut_b, blocks, inside, 0)
    share.wait_send()
    remote(into.at[core], into.at[1 - core], send_c, recv_c, {"seq": sibling}).wait_recv()

    for d, edge in ((0, first_doc), (1, last_doc)):
        for g in range(2):
            part = slice(g * half, (g + 1) * half)

            @pl.when(core == d)
            def _(d=d, g=g, part=part, edge=edge):
                same = (into[g, d, 129:130, :] == edge).astype(F32)
                state[d, :, part] = into[g, d, 0:128, :] * same

            @pl.when(core != d)
            def _(d=d, g=g, part=part, edge=edge):
                top, end = join(other[g, d], into[g, d])
                state[d, :, part] = top * (end[1:2] == edge).astype(F32)

    def leave(d, k):
        before = state[d]
        given = jnp.dot(maps_ref[2 * d + 1, at(k), :], before.astype(BF16), preferred_element_type=F32)
        state[d] = before * gains[k, d : d + 1, :] + local[d, k]
        return given * spread(columns[at(k), :], (4 + d) * heads, heads)

    def forward(k, carry):
        acc[at(k), :] += leave(0, k)
        return carry

    lax.fori_loop(0, blocks, forward, 0)
    inverse[...] = jnp.zeros((BLOCK, 128), F32)
    skip = jnp.concatenate([skip_ref[...], jnp.zeros((1, 128 - heads), F32)], axis=1)
    skip = spread(jnp.broadcast_to(skip, (8, 128)), 0, heads)[:1]
    lane = iota((BLOCK, 128), 1)

    def backward(step, carry):
        k = blocks - 1 - step
        part = leave(1, k)
        gate = gate_ref[at(k), :].astype(F32)
        mixed = acc[at(k), :] + part + skip * x_ref[at(k), :].astype(F32)
        gated = mixed * (gate / (1.0 + jnp.exp(-gate)))
        acc[at(k), :] = gated
        inverse[...] += jnp.where(lane == k, jnp.sum(gated * gated, axis=1, keepdims=True), 0.0)
        return carry

    lax.fori_loop(0, blocks, backward, 0)
    kept = squares.shape[1]
    squares[0] = inverse[...].T[0:kept]
    to_heads = [
        remote(squares.at[0], squares.at[o], send_h.at[o], recv_h.at[o], head_at(o))
        for o in range(1, head_ways)
    ]
    for copy in to_heads:
        copy.start()
    for copy in to_heads:
        copy.wait()
    sum_all = squares[0]
    for o in range(1, head_ways):
        sum_all = sum_all + squares[o]
    rest = jnp.zeros((BLOCK - kept, 128), F32)
    root = lax.rsqrt(sum_all / (head_ways * width) + 1e-05)
    inverse[...] = jnp.concatenate([root, rest], axis=0).T

    def scale(k, carry):
        factor = jnp.sum(jnp.where(lane == k, inverse[...], 0.0), axis=1, keepdims=True)
        out_ref[at(k), :] = (acc[at(k), :] * factor * gain_ref[...]).astype(BF16)
        return carry

    lax.fori_loop(0, blocks, scale, 0)


def local(
    mixer_input, gate_input, state_maps, step_size, log_decay, skip_weight, doc_ids, norm_gain
):
    tokens, width = mixer_input.shape
    heads = step_size.shape[1]
    blocks = tokens // BLOCK
    half = width // 2
    seq, head_ways = lax.axis_size("seq"), lax.axis_size("head")
    chips = seq // 2
    docs = doc_ids.reshape(blocks, BLOCK)
    vmem = pl.BlockSpec(memory_space=pltpu.VMEM)
    return pl.pallas_call(
        functools.partial(kernel, (seq, head_ways, heads)),
        out_shape=jax.ShapeDtypeStruct((tokens, width), BF16),
        in_specs=[vmem] * 8,
        out_specs=vmem,
        scratch_shapes=[
            pltpu.VMEM((2, 2, ROWS, half), F32),
            pltpu.VMEM((2, 2, ROWS, half), F32),
            pltpu.VMEM((2, ROWS, half), F32),
            pltpu.VMEM((chips, ROWS, half), F32),
            pltpu.VMEM((2, 2, ROWS, half), F32),
            pltpu.VMEM((2, blocks, 128, width), F32),
            pltpu.VMEM((tokens, 128), F32),
            pltpu.VMEM((blocks, 2, heads, 128), F32),
            pltpu.VMEM((blocks, 2, width), F32),
            pltpu.VMEM((2, 128, width), F32),
            pltpu.VMEM((tokens, width), F32),
            pltpu.VMEM((head_ways, -(-blocks // 8) * 8, 128), F32),
            pltpu.VMEM((BLOCK, 128), F32),
            pltpu.SemaphoreType.DMA,
            pltpu.SemaphoreType.DMA,
            pltpu.SemaphoreType.DMA((chips,)),
            pltpu.SemaphoreType.DMA((chips,)),
            pltpu.SemaphoreType.DMA,
            pltpu.SemaphoreType.DMA,
            pltpu.SemaphoreType.DMA((head_ways,)),
            pltpu.SemaphoreType.DMA((head_ways,)),
        ],
        compiler_params=pltpu.CompilerParams(
            collective_id=0, has_side_effects=True, vmem_limit_bytes=56 * 2**20
        ),
    )(mixer_input, gate_input, state_maps, step_size, log_decay, skip_weight[None, :], docs, norm_gain[None, :])


def solution(mesh):
    return jax.shard_map(
        local,
        mesh=mesh,
        in_specs=(
            P("seq", "head"),
            P("seq", "head"),
            P(None, "seq", None),
            P(None, "head", "seq"),
            P(None, "head", "seq"),
            P("head"),
            P("seq"),
            P("head"),
        ),
        out_specs=P("seq", "head"),
        check_vma=False,
    )
```

```python
import functools

import jax
import jax.numpy as jnp
from jax import lax
from jax.experimental import pallas as pl
from jax.experimental.pallas import tpu as pltpu
from jax.sharding import PartitionSpec as P

BLOCK = 128
ROWS = 136
F32 = jnp.float32
BF16 = jnp.bfloat16
HIGH = lax.Precision.HIGHEST


def iota(shape, axis):
    return lax.broadcasted_iota(jnp.int32, shape, axis)


def spread(columns, first, heads):
    rows = columns.shape[0]
    half = iota((rows, 128), 1) // 64
    parts = []
    for pair in range(heads // 2):
        index = first + 2 * pair + half
        parts.append(jnp.take_along_axis(columns, index, axis=1, mode="promise_in_bounds"))
    return jnp.concatenate(parts, axis=1)


def kernel(
    sizes, x_ref, gate_hbm, maps_ref, step_ref, decay_ref, skip_ref, docs_ref, gain_ref, out_hbm,
    own, other, total, slots, into, local, columns, rows, gains, state, acc, squares, inverse, gate_ref, silu, out_ref,
    gate_sem, out_sems, send_a, recv_a, send_b, recv_b, send_c, recv_c, send_h, recv_h,
):
    seq, head_ways, heads = sizes
    chips = seq // 2
    width = heads * 64
    half = width // 2
    blocks = x_ref.shape[0] // BLOCK
    place = lax.axis_index("seq")
    core = lax.rem(place, 2)
    chip = lax.div(place, 2)
    head_place = lax.axis_index("head")
    sibling = place + 1 - 2 * core

    def chip_at(offset):
        return {"seq": 2 * lax.rem(chip + offset, chips) + core}

    def head_at(offset):
        return {"head": lax.rem(head_place + offset, head_ways)}

    gate_copy = pltpu.make_async_copy(gate_hbm, gate_ref, gate_sem)
    gate_copy.start()
    barrier = pltpu.get_barrier_semaphore()
    partners = [{"seq": sibling}]
    partners += [chip_at(o) for o in range(1, chips)] + [head_at(o) for o in range(1, head_ways)]
    for partner in partners:
        pl.semaphore_signal(barrier, inc=1, device_id=partner, device_id_type=pl.DeviceIdType.MESH)
    pl.semaphore_wait(barrier, len(partners))

    def remote(src, dst, send, recv, device):
        return pltpu.make_async_remote_copy(
            src_ref=src, dst_ref=dst, send_sem=send, recv_sem=recv,
            device_id=device, device_id_type=pl.DeviceIdType.MESH,
        )

    below = (iota((BLOCK, BLOCK), 0) <= iota((BLOCK, BLOCK), 1)).astype(F32)
    above = (iota((BLOCK, BLOCK), 0) >= iota((BLOCK, BLOCK), 1)).astype(F32)
    tile = iota((8, half), 0)

    def at(k):
        return pl.ds(pl.multiple_of(k * BLOCK, BLOCK), BLOCK)

    state[...] = jnp.zeros_like(state)
    first_doc = docs_ref[0:1, :].astype(F32)[:, :1]
    last_doc = docs_ref[blocks - 1 : blocks, :].astype(F32)[:, BLOCK - 1 :]

    def summarize(k, carry):
        log_f, log_b, prior = carry
        docs = docs_ref[pl.ds(k, 1), :].astype(F32)
        after = docs_ref[pl.ds(jnp.minimum(k + 1, blocks - 1), 1), :].astype(F32)
        first, last = docs[:, :1], docs[:, BLOCK - 1 :]
        after = jnp.where(k == blocks - 1, last, after[:, :1])
        cum_f = jnp.dot(decay_ref[0, :, at(k)], below, precision=HIGH, preferred_element_type=F32)
        cum_b = jnp.dot(decay_ref[1, :, at(k)], above, precision=HIGH, preferred_element_type=F32)
        step_f, step_b = step_ref[0, :, at(k)], step_ref[1, :, at(k)]
        in_f = jnp.where(docs == last, jnp.exp(cum_f[:, BLOCK - 1 :] - cum_f) * step_f, 0.0)
        in_b = jnp.where(docs == first, jnp.exp(cum_b[:, :1] - cum_b) * step_b, 0.0)
        out_f = jnp.where(docs == prior, jnp.exp(cum_f), 0.0)
        out_b = jnp.where(docs == after, jnp.exp(cum_b), 0.0)
        pad = jnp.zeros((BLOCK - 6 * heads, BLOCK), F32)
        cols = jnp.concatenate([cum_f, cum_b, in_f, in_b, out_f, out_b, pad], axis=0).T
        columns[at(k), :] = cols
        rows[k, 0] = cum_f - jnp.log(step_f)
        rows[k, 1] = cum_b - jnp.log(step_b)
        x = x_ref[at(k), :].astype(F32)
        put_f = (x * spread(cols, 2 * heads, heads)).astype(BF16)
        put_b = (x * spread(cols, 3 * heads, heads)).astype(BF16)
        map_f = maps_ref[0, at(k), :].astype(F32).T.astype(BF16)
        map_b = maps_ref[2, at(k), :].astype(F32).T.astype(BF16)
        local_f = jnp.dot(map_f, put_f, preferred_element_type=F32)
        local_b = jnp.dot(map_b, put_b, preferred_element_type=F32)
        local[0, k] = local_f
        local[1, k] = local_b
        block_f = spread(cols[BLOCK - 8 :], 0, heads)[7:]
        block_b = spread(cols[:8], heads, heads)[:1]
        keep = jnp.exp(block_f) * (prior == last).astype(F32)
        gains[k, 0:1, :] = keep
        gains[k, 1:2, :] = jnp.exp(block_b) * (after == first).astype(F32)
        state[0] = state[0] * keep + local_f
        state[1] = state[1] + local_b * (jnp.exp(log_b) * (first == first_doc).astype(F32))
        return log_f + block_f, log_b + block_b, last

    zero = jnp.zeros((1, width), F32)
    logs = lax.fori_loop(0, blocks, summarize, (zero, zero, first_doc))
    for g in range(2):
        part = slice(g * half, (g + 1) * half)
        for d, doc in ((0, last_doc), (1, first_doc)):
            own[g, d, 0:128, :] = state[d, :, part]
            own[g, d, 128:ROWS, :] = jnp.where(tile == 0, logs[d][:, part], doc)

    to_sibling = remote(own, other, send_a, recv_a, {"seq": sibling})
    to_sibling.start()

    low = iota((BLOCK, BLOCK), 1) < iota((BLOCK, BLOCK), 0)
    diagonal = iota((BLOCK, BLOCK), 1) == iota((BLOCK, BLOCK), 0)
    left = iota((BLOCK, BLOCK), 1) < 64
    skip = jnp.concatenate([skip_ref[...], jnp.zeros((1, 128 - heads), F32)], axis=1)
    skip = spread(jnp.broadcast_to(skip, (8, 128)), 0, heads)[:1]
    lane = iota((BLOCK, 128), 1)
    gate_copy.wait()

    def inside(k, carry):
        docs = jnp.broadcast_to(docs_ref[pl.ds(k, 1), :].astype(F32), (BLOCK, BLOCK))
        dims = (((1,), (1,)), ((), ()))
        score_f = lax.dot_general(maps_ref[1, at(k), :], maps_ref[0, at(k), :], dims, preferred_element_type=F32)
        score_b = lax.dot_general(maps_ref[3, at(k), :], maps_ref[2, at(k), :], dims, preferred_element_type=F32)
        same = (docs == docs.T) & jnp.logical_not(diagonal)
        score = jnp.where(same, jnp.where(low, score_f, score_b), 0.0)
        cols = columns[at(k), :]
        row_f, row_b = rows[k, 0], rows[k, 1]
        for pair in range(heads // 2):
            lanes = slice(pair * 128, pair * 128 + 128)
            x = x_ref[at(k), lanes]
            weights = []
            for h in (2 * pair, 2 * pair + 1):
                power = jnp.where(
                    low,
                    cols[:, h : h + 1] - row_f[h : h + 1],
                    cols[:, heads + h : heads + h + 1] - row_b[h : h + 1],
                )
                weights.append((score * jnp.exp(power)).astype(BF16))
            none = jnp.zeros_like(x)
            values = jnp.concatenate([jnp.where(left, x, none), jnp.where(left, none, x)], axis=0)
            acc[at(k), lanes] = skip[:, lanes] * x.astype(F32) + jnp.dot(
                jnp.concatenate(weights, axis=1), values, preferred_element_type=F32
            )
            gate = gate_ref[at(k), lanes].astype(F32)
            silu[at(k), lanes] = gate / (1.0 + jnp.exp(-gate))
        return carry

    cut_a, cut_b = blocks // 4, blocks - blocks // 6
    lax.fori_loop(0, cut_a, inside, 0)
    to_sibling.wait()

    def join(later, earlier):
        log, doc = later[128:129], later[129:130]
        keep = jnp.exp(log) * (doc == earlier[129:130]).astype(F32)
        top = later[0:128] + keep * earlier[0:128]
        return top, jnp.where(tile == 0, log + earlier[128:129], doc)

    @pl.when(core == 0)
    def _():
        for d, (later, earlier) in ((0, (other, own)), (1, (own, other))):
            top, end = join(later[0, d], earlier[0, d])
            total[d, 0:128, :] = top
            total[d, 128:ROWS, :] = end

    @pl.when(core == 1)
    def _():
        for d, (later, earlier) in ((0, (own, other)), (1, (other, own))):
            top, end = join(later[1, d], earlier[1, d])
            total[d, 0:128, :] = top
            total[d, 128:ROWS, :] = end

    to_chips = []
    for o in range(1, chips):
        way = jnp.where(chip + o < chips, 0, 1)
        to_chips.append(remote(total.at[way], slots.at[o], send_b.at[o], recv_b.at[o], chip_at(o)))
        to_chips[-1].start()
    lax.fori_loop(cut_a, cut_b, inside, 0)
    for copy in to_chips:
        copy.wait()

    for d in range(2):
        into[core, d, 0:128, :] = jnp.zeros((128, half), F32)
        into[core, d, 128:ROWS, :] = jnp.where(tile == 0, 0.0, -1.0)
        for o in range(1, chips):
            slot = o if d == 0 else chips - o
            there = chip >= o if d == 0 else chip + o < chips

            @pl.when(there)
            def _(d=d, o=o, slot=slot):
                part = slots[slot]
                log, doc = part[128:129], part[129:130]
                if o == 1:
                    into[core, d] = part
                else:
                    so_far = into[core, d, 128:ROWS, :]
                    keep = jnp.exp(so_far[0:1]) * (doc == so_far[1:2]).astype(F32)
                    into[core, d, 0:128, :] += keep * part[0:128]
                    into[core, d, 128:ROWS, :] = jnp.where(tile == 0, so_far[0:1] + log, so_far[1:2])

    share = remote(into.at[core], into.at[core], send_c, recv_c, {"seq": sibling})
    share.start()
    lax.fori_loop(cut_b, blocks, inside, 0)
    share.wait_send()
    remote(into.at[core], into.at[1 - core], send_c, recv_c, {"seq": sibling}).wait_recv()

    for d, edge in ((0, first_doc), (1, last_doc)):
        for g in range(2):
            part = slice(g * half, (g + 1) * half)

            @pl.when(core == d)
            def _(d=d, g=g, part=part, edge=edge):
                same = (into[g, d, 129:130, :] == edge).astype(F32)
                state[d, :, part] = into[g, d, 0:128, :] * same

            @pl.when(core != d)
            def _(d=d, g=g, part=part, edge=edge):
                top, end = join(other[g, d], into[g, d])
                state[d, :, part] = top * (end[1:2] == edge).astype(F32)

    def leave(d, k):
        before = state[d]
        given = jnp.dot(maps_ref[2 * d + 1, at(k), :], before.astype(BF16), preferred_element_type=F32)
        state[d] = before * gains[k, d : d + 1, :] + local[d, k]
        return given * spread(columns[at(k), :], (4 + d) * heads, heads)

    def forward(k, carry):
        acc[at(k), :] += leave(0, k)
        return carry

    lax.fori_loop(0, blocks, forward, 0)
    inverse[...] = jnp.zeros((BLOCK, 128), F32)

    def backward(step, carry):
        k = blocks - 1 - step
        part = leave(1, k)
        gated = (acc[at(k), :] + part) * silu[at(k), :]
        acc[at(k), :] = gated
        inverse[...] += jnp.where(lane == k, jnp.sum(gated * gated, axis=1, keepdims=True), 0.0)
        return carry

    lax.fori_loop(0, blocks, backward, 0)
    kept = squares.shape[1]
    squares[0] = inverse[...].T[0:kept]
    to_heads = [
        remote(squares.at[0], squares.at[o], send_h.at[o], recv_h.at[o], head_at(o))
        for o in range(1, head_ways)
    ]
    for copy in to_heads:
        copy.start()
    for copy in to_heads:
        copy.wait()
    sum_all = squares[0]
    for o in range(1, head_ways):
        sum_all = sum_all + squares[o]
    rest = jnp.zeros((BLOCK - kept, 128), F32)
    root = lax.rsqrt(sum_all / (head_ways * width) + 1e-05)
    inverse[...] = jnp.concatenate([root, rest], axis=0).T

    def scale(k, carry):
        factor = jnp.sum(jnp.where(lane == k, inverse[...], 0.0), axis=1, keepdims=True)
        out_ref[at(k), :] = (acc[at(k), :] * factor * gain_ref[...]).astype(BF16)
        pltpu.make_async_copy(out_ref.at[at(k)], out_hbm.at[at(k)], out_sems.at[k]).start()
        return carry

    def drain(k, carry):
        pltpu.make_async_copy(out_ref.at[at(k)], out_hbm.at[at(k)], out_sems.at[k]).wait()
        return carry

    lax.fori_loop(0, blocks, scale, 0)
    lax.fori_loop(0, blocks, drain, 0)


def local(
    mixer_input, gate_input, state_maps, step_size, log_decay, skip_weight, doc_ids, norm_gain
):
    tokens, width = mixer_input.shape
    heads = step_size.shape[1]
    blocks = tokens // BLOCK
    half = width // 2
    seq, head_ways = lax.axis_size("seq"), lax.axis_size("head")
    chips = seq // 2
    docs = doc_ids.reshape(blocks, BLOCK)
    vmem = pl.BlockSpec(memory_space=pltpu.VMEM)
    hbm = pl.BlockSpec(memory_space=pl.ANY)
    return pl.pallas_call(
        functools.partial(kernel, (seq, head_ways, heads)),
        out_shape=jax.ShapeDtypeStruct((tokens, width), BF16),
        in_specs=[vmem, hbm] + [vmem] * 6,
        out_specs=hbm,
        scratch_shapes=[
            pltpu.VMEM((2, 2, ROWS, half), F32),
            pltpu.VMEM((2, 2, ROWS, half), F32),
            pltpu.VMEM((2, ROWS, half), F32),
            pltpu.VMEM((chips, ROWS, half), F32),
            pltpu.VMEM((2, 2, ROWS, half), F32),
            pltpu.VMEM((2, blocks, 128, width), F32),
            pltpu.VMEM((tokens, 128), F32),
            pltpu.VMEM((blocks, 2, heads, 128), F32),
            pltpu.VMEM((blocks, 2, width), F32),
            pltpu.VMEM((2, 128, width), F32),
            pltpu.VMEM((tokens, width), F32),
            pltpu.VMEM((head_ways, -(-blocks // 8) * 8, 128), F32),
            pltpu.VMEM((BLOCK, 128), F32),
            pltpu.VMEM((tokens, width), BF16),
            pltpu.VMEM((tokens, width), F32),
            pltpu.VMEM((tokens, width), BF16),
            pltpu.SemaphoreType.DMA,
            pltpu.SemaphoreType.DMA((blocks,)),
            pltpu.SemaphoreType.DMA,
            pltpu.SemaphoreType.DMA,
            pltpu.SemaphoreType.DMA((chips,)),
            pltpu.SemaphoreType.DMA((chips,)),
            pltpu.SemaphoreType.DMA,
            pltpu.SemaphoreType.DMA,
            pltpu.SemaphoreType.DMA((head_ways,)),
            pltpu.SemaphoreType.DMA((head_ways,)),
        ],
        compiler_params=pltpu.CompilerParams(
            collective_id=0, has_side_effects=True, vmem_limit_bytes=56 * 2**20
        ),
    )(mixer_input, gate_input, state_maps, step_size, log_decay, skip_weight[None, :], docs, norm_gain[None, :])


def solution(mesh):
    return jax.shard_map(
        local,
        mesh=mesh,
        in_specs=(
            P("seq", "head"),
            P("seq", "head"),
            P(None, "seq", None),
            P(None, "head", "seq"),
            P(None, "head", "seq"),
            P("head"),
            P("seq"),
            P("head"),
        ),
        out_specs=P("seq", "head"),
        check_vma=False,
    )
```
